32 devices in a mesh: parts: 2 (over x), serve: 2 (over core), tensor: 8 (over z, y).
Axes of the slice: x: 2, y: 2, z: 4, core: 2. Of those that a mesh axis runs over, the one named last changes fastest.
Arguments:
- activations: bfloat16 [2, 1536, 8192], P(None, ('parts', 'serve'), 'tensor'), parts along dimension 1, may hold values from -6 to 6
- shared_weight_matrix: bfloat16 [8192, 8192], P('tensor'), may hold values from -0.0625 to 0.0625
- adapter_down_weight: bfloat16 [16, 8192, 128], P('serve', 'tensor'), may hold values from -0.0625 to 0.0625
- adapter_up_weight: bfloat16 [16, 128, 8192], P('serve', None, 'tensor'), may hold values from -0.5 to 0.5
- adapter_rank_scale: bfloat16 [16, 128], P('serve'), may hold values from 0.5 to 2
- block_adapter_index: int32 [12], P('parts'), parts along dimension 0, may hold values from 0 to 15, as said below
Outputs:
- projected: bfloat16 [2, 1536, 8192], P(None, ('parts', 'serve'), 'tensor'), parts along dimension 1
The draws below stay inside these ranges and needn't reach their ends.
There are 2 independent parts, one for each index of `parts`. The reference program is written for one: setup_inputs(seed, part) draws one part's arguments, and reference() takes and returns one part's arrays. A program takes and returns all parts, laid end to end along the dimension named above; an argument that names none is the same for every part. Nothing has to cross between parts.
Inputs may be any that keep to these rules, and one draw needn't show every extreme that they name: `block_adapter_index`: each entry names the variant of one block of 128 rows; the first two blocks name different variants.
All inputs are finite; a program needn't handle non-finite values.
Results may differ from the reference program's by a relative error of at most 0.004.
Values may be sent and summed in bfloat16 or wider, within the bound.
A program may use at most 192 MiB of HBM per device.

```python
import math
import jax
import jax.numpy as jnp

MODEL_WIDTH = 8192
DELTA_RANK = 128
ADAPTER_COUNT = 16
BLOCK = 128
STEPS = 2
BLOCKS = 6
ROWS = 768


def draw_block_adapter_index(key, part):
    key = jax.random.fold_in(key, 7)
    key_order, key_first, key_second, key_other = jax.random.split(key, 4)
    order = jax.random.permutation(key_order, ADAPTER_COUNT).astype(jnp.int32)
    first_pick = jax.random.randint(key_first, (BLOCKS,), 0, ADAPTER_COUNT)
    second_pick = jax.random.randint(key_second, (BLOCKS,), 0, ADAPTER_COUNT)
    skewed = order[jnp.minimum(first_pick, second_pick)].astype(jnp.int32)
    lead = (ADAPTER_COUNT - 1 - part) % ADAPTER_COUNT
    follow = (lead + 1 + jax.random.randint(key_other, (), 0, ADAPTER_COUNT - 1)) % ADAPTER_COUNT
    position = jnp.arange(BLOCKS)
    chosen = jnp.where(position == 0, lead, jnp.where(position == 1, follow, skewed))
    return chosen.astype(jnp.int32)


def shard_levels(stream_key, dims, cuts, smallest, high):
    factor_of = 1.0
    for dim, parts in cuts:
        draws = jax.random.uniform(jax.random.fold_in(jax.random.fold_in(stream_key, 6), dim), (parts,), jnp.float32, smallest / len(cuts), high / len(cuts))
        factor_of = factor_of * jnp.repeat(jnp.exp(draws), dims[dim] // parts).reshape((-1,) + (1,) * (len(dims) - 1 - dim))
    return factor_of


def bell_draw(stream_key, shape, scale, limit, shards=(), held_as=jnp.bfloat16):
    drawn = jax.random.normal(stream_key, shape, jnp.float32) * scale
    if len(shards) > 0:
        drawn = shard_levels(stream_key, shape, shards, -0.22, 0.18) * drawn
    return jnp.clip(drawn, min=-limit, max=limit).astype(held_as)


def setup_inputs(seed: int = 0, part: int = 0) -> dict:
    keys = jax.random.split(jax.random.key(seed), 7)
    part_keys = jax.random.split(jax.random.fold_in(keys[6], part), 7)
    return {
        "activations": bell_draw(part_keys[0], (STEPS, ROWS, MODEL_WIDTH), 1.0, 6.0, ((1, 2), (2, 8))),
        "shared_weight_matrix": bell_draw(keys[1], (MODEL_WIDTH, MODEL_WIDTH), MODEL_WIDTH ** -0.5, 0.0625, ((0, 8),)),
        "adapter_down_weight": bell_draw(keys[2], (ADAPTER_COUNT, MODEL_WIDTH, DELTA_RANK), MODEL_WIDTH ** -0.5, 0.0625, ((0, 2), (1, 8))),
        "adapter_up_weight": bell_draw(keys[3], (ADAPTER_COUNT, DELTA_RANK, MODEL_WIDTH), DELTA_RANK ** -0.5, 0.5, ((0, 2), (2, 8))),
        "adapter_rank_scale": jnp.clip(jnp.exp(math.log(2.0) - 1.3862944 * jax.random.uniform(keys[4], (ADAPTER_COUNT, DELTA_RANK), jnp.float32) ** shard_levels(keys[4], (ADAPTER_COUNT, DELTA_RANK), ((0, 2),), -0.2, 0.2)), 0.5, 2.0).astype(jnp.bfloat16),
        "block_adapter_index": draw_block_adapter_index(jax.random.fold_in(jax.random.fold_in(keys[6], part), 71), part),
    }


def reference(activations, shared_weight_matrix, adapter_down_weight, adapter_up_weight, adapter_rank_scale, block_adapter_index):
    base = jnp.einsum('srd,de->sre', activations.astype(jnp.float32), shared_weight_matrix.astype(jnp.float32))
    selected_down_factor = jnp.take(adapter_down_weight, block_adapter_index, axis=0).astype(jnp.float32)
    selected_up_factor = jnp.take(adapter_up_weight, block_adapter_index, axis=0).astype(jnp.float32)
    selected_scale = jnp.take(adapter_rank_scale, block_adapter_index, axis=0).astype(jnp.float32)
    blocked = activations.reshape(STEPS, BLOCKS, BLOCK, MODEL_WIDTH).astype(jnp.float32)
    rank_sum = jnp.einsum('sbkd,bdr->sbkr', blocked, selected_down_factor)
    rank_scaled = (rank_sum * selected_scale[None, :, None, :]).astype(jnp.bfloat16)
    delta = jnp.einsum('sbkr,brc->sbkc', rank_scaled.astype(jnp.float32), selected_up_factor).reshape(STEPS, ROWS, MODEL_WIDTH)
    return (base + delta).astype(jnp.bfloat16)
```

```python
import functools

import jax
import jax.numpy as jnp
from jax import lax
from jax.experimental import pallas as pl
from jax.experimental.pallas import tpu as pltpu
from jax.sharding import PartitionSpec as P

BLOCK = 128
TILE_ROWS = 128
MESH = pl.DeviceIdType.MESH


def chunk_at(step, place, length):
    after, before = length - 1 - place, place
    fewer = jnp.minimum(after, before)
    after_more = after > before
    interleaved = step < 2 * fewer
    count = jnp.where(interleaved, step // 2, step - fewer)
    goes_after = jnp.where(interleaved & (step % 2 == 1), jnp.logical_not(after_more), after_more)
    chunk = jnp.where(goes_after, length - 1 - count, count)
    return jnp.where(step == length - 1, place, chunk)


def base_kernel(
    length,
    x_ref,
    w_ref,
    out_ref,
    x_pair,
    w_own,
    w_pair,
    acc,
    own_sem,
    x_send,
    x_recv,
    y_send,
    y_recv,
    across_send,
    across_recv,
    core_send,
    core_recv,
    chain_send,
    chain_recv,
):
    tiles, rows, width = x_ref.shape
    part, group, index = lax.axis_index("parts"), lax.axis_index("serve"), lax.axis_index("tensor")
    side, place = index % 2, index // 2
    twin = index + 1 - 2 * side
    other_part = part + 1 - 2 * (part % 2)
    other_group = 1 - group
    quarter = width // 4
    mine = pl.multiple_of((2 * (part % 2) + group) * quarter, quarter)
    across = pl.multiple_of((2 * (other_part % 2) + group) * quarter, quarter)

    def columns(chunk, which):
        return pl.ds(pl.multiple_of((2 * chunk + which) * width, width), width)

    def own_copy(step):
        chunk = chunk_at(step, place, length)
        return pltpu.make_async_copy(
            w_ref.at[:, columns(chunk, side)], w_own.at[chunk], own_sem.at[chunk]
        )

    def x_copy(tile):
        return pltpu.make_async_remote_copy(
            src_ref=x_ref.at[tile],
            dst_ref=x_pair.at[tile],
            send_sem=x_send.at[tile],
            recv_sem=x_recv.at[tile],
            device_id={"tensor": twin},
            device_id_type=MESH,
        )

    def y_copy(step):
        chunk = chunk_at(step, place, length)
        return pltpu.make_async_remote_copy(
            src_ref=w_ref.at[pl.ds(mine, quarter), columns(chunk, 1 - side)],
            dst_ref=w_pair.at[chunk, pl.ds(mine, quarter), :],
            send_sem=y_send.at[chunk],
            recv_sem=y_recv.at[chunk],
            device_id={"tensor": twin},
            device_id_type=MESH,
        )

    def across_copy(step):
        chunk = chunk_at(step, place, length)
        block = w_pair.at[chunk, pl.ds(mine, quarter), :]
        return pltpu.make_async_remote_copy(
            src_ref=block,
            dst_ref=block,
            send_sem=across_send.at[chunk],
            recv_sem=across_recv.at[chunk],
            device_id={"parts": other_part},
            device_id_type=MESH,
        )

    def core_copy(step, which, start):
        chunk = chunk_at(step, place, length)
        block = w_pair.at[chunk, pl.ds(start, quarter), :]
        return pltpu.make_async_remote_copy(
            src_ref=block,
            dst_ref=block,
            send_sem=core_send.at[which, chunk],
            recv_sem=core_recv.at[which, chunk],
            device_id={"serve": other_group},
            device_id_type=MESH,
        )

    def chain_copy(chunk, tile, slot, target):
        return pltpu.make_async_remote_copy(
            src_ref=acc.at[chunk, tile],
            dst_ref=acc.at[slot, tile],
            send_sem=chain_send.at[chunk, tile],
            recv_sem=chain_recv.at[slot, tile],
            device_id={"tensor": target},
            device_id_type=MESH,
        )

    def forward_first(step):
        y_copy(step).wait_recv()
        across_copy(step).start()
        core_copy(step, 0, mine).start()

    def forward_second(step):
        across_copy(step).wait_recv()
        core_copy(step, 1, across).start()

    @pl.loop(0, length)
    def _(step):
        own_copy(step).start()

    barrier = pltpu.get_barrier_semaphore()
    pl.semaphore_signal(barrier, inc=1, device_id={"tensor": twin}, device_id_type=MESH)
    pl.semaphore_signal(barrier, inc=1, device_id={"parts": other_part}, device_id_type=MESH)
    pl.semaphore_signal(barrier, inc=1, device_id={"serve": other_group}, device_id_type=MESH)

    @pl.when(place > 0)
    def _():
        pl.semaphore_signal(barrier, inc=1, device_id={"tensor": index - 2}, device_id_type=MESH)

    @pl.when(place < length - 1)
    def _():
        pl.semaphore_signal(barrier, inc=1, device_id={"tensor": index + 2}, device_id_type=MESH)

    at_end = (place == 0) | (place == length - 1)
    pl.semaphore_wait(barrier, jnp.where(at_end, 4, 5))

    y_copy(0).start()

    @pl.loop(0, tiles)
    def _(tile):
        x_copy(tile).start()

    @pl.loop(1, length)
    def _(step):
        y_copy(step).start()

    forward_first(0)
    forward_second(0)

    @pl.loop(0, length)
    def _(step):
        chunk = chunk_at(step, place, length)
        own_copy(step).wait()
        core_copy(step, 0, mine).wait_recv()
        core_copy(step, 1, across).wait_recv()

        @pl.loop(0, tiles)
        def _(tile):
            @pl.when(step == 0)
            def _():
                x_copy(tile).wait_recv()

            part_sum = jnp.dot(
                x_ref[tile], w_own[chunk], preferred_element_type=jnp.float32
            ) + jnp.dot(x_pair[tile], w_pair[chunk], preferred_element_type=jnp.float32)

            @pl.when(chunk == place)
            def _():
                out_ref[tile] = part_sum

                @pl.when(place > 0)
                def _():
                    chain_copy(chunk, tile, chunk, index).wait_recv()
                    out_ref[tile] += acc[chunk, tile].astype(jnp.float32)

                @pl.when(place < length - 1)
                def _():
                    chain_copy(chunk, tile, length, index).wait_recv()
                    out_ref[tile] += acc[length, tile].astype(jnp.float32)

            @pl.when(chunk != place)
            def _():
                up = chunk > place
                first = jnp.where(up, place == 0, place == length - 1)

                @pl.when(first)
                def _():
                    acc[chunk, tile] = part_sum.astype(acc.dtype)

                @pl.when(jnp.logical_not(first))
                def _():
                    chain_copy(chunk, tile, chunk, index).wait_recv()
                    acc[chunk, tile] = (part_sum + acc[chunk, tile].astype(jnp.float32)).astype(
                        acc.dtype
                    )

                target = jnp.where(up, index + 2, index - 2)
                slot = jnp.where(chunk == place - 1, length, chunk)
                chain_copy(chunk, tile, slot, target).start()

            @pl.when((step < length - 1) & (tile == tiles // 2))
            def _():
                forward_first(step + 1)

            @pl.when((step < length - 1) & (tile == tiles - 1))
            def _():
                forward_second(step + 1)

    @pl.loop(0, tiles)
    def _(tile):
        x_copy(tile).wait_send()

    @pl.loop(0, length)
    def _(step):
        y_copy(step).wait_send()
        across_copy(step).wait_send()
        core_copy(step, 0, mine).wait_send()
        core_copy(step, 1, across).wait_send()

        chunk = chunk_at(step, place, length)

        @pl.when(chunk != place)
        def _():
            @pl.loop(0, tiles)
            def _(tile):
                chain_copy(chunk, tile, chunk, index).wait_send()


def base_sum(activations, shared_weight_matrix, length):
    row_count, width = activations.shape
    tiles = row_count // TILE_ROWS
    dma = pltpu.SemaphoreType.DMA
    return pl.pallas_call(
        functools.partial(base_kernel, length),
        out_shape=jax.ShapeDtypeStruct((tiles, TILE_ROWS, width), jnp.float32),
        in_specs=[
            pl.BlockSpec(memory_space=pltpu.VMEM),
            pl.BlockSpec(memory_space=pl.ANY),
        ],
        out_specs=pl.BlockSpec(memory_space=pltpu.VMEM),
        scratch_shapes=[
            pltpu.VMEM((tiles, TILE_ROWS, width), jnp.bfloat16),
            pltpu.VMEM((length, width, width), jnp.bfloat16),
            pltpu.VMEM((length, width, width), jnp.bfloat16),
            pltpu.VMEM((length + 1, tiles, TILE_ROWS, width), jnp.bfloat16),
            dma((length,)),
            dma((tiles,)),
            dma((tiles,)),
            dma((length,)),
            dma((length,)),
            dma((length,)),
            dma((length,)),
            dma((2, length)),
            dma((2, length)),
            dma((length, tiles)),
            dma((length + 1, tiles)),
        ],
        compiler_params=pltpu.CompilerParams(
            collective_id=0, has_side_effects=True, vmem_limit_bytes=52 * 2**20
        ),
        cost_estimate=pl.CostEstimate(
            flops=4 * row_count * width * width * length * 8,
            bytes_accessed=2 * width * width * length * 2 * 8,
            transcendentals=0,
        ),
        name="base_sum",
    )(activations.reshape(tiles, TILE_ROWS, width), shared_weight_matrix)


def pick_rows(table, served, group_index):
    held = table.shape[0]
    count = served.shape[0] // 2
    local = served - group_index * held
    here = (local >= 0) & (local < held)
    local = jnp.clip(local, 0, held - 1)
    ours = lax.dynamic_slice_in_dim(local, group_index * count, count)
    ours_here = lax.dynamic_slice_in_dim(here, group_index * count, count)
    theirs = lax.dynamic_slice_in_dim(local, (1 - group_index) * count, count)
    sent = jnp.take(table, theirs, axis=0)
    arrived = lax.ppermute(sent, "serve", [(0, 1), (1, 0)])
    kept = jnp.take(table, ours, axis=0)
    shape = (count,) + (1,) * (table.ndim - 1)
    return jnp.where(ours_here.reshape(shape), kept, arrived)


def per_device(
    length,
    activations,
    shared_weight_matrix,
    adapter_down_weight,
    adapter_up_weight,
    adapter_rank_scale,
    block_adapter_index,
):
    step_count, row_count, width_dev = activations.shape
    block_count = row_count // BLOCK
    group_index = lax.axis_index("serve")
    down = pick_rows(adapter_down_weight, block_adapter_index, group_index)
    up = pick_rows(adapter_up_weight, block_adapter_index, group_index)
    scale = pick_rows(adapter_rank_scale, block_adapter_index, group_index)
    blocked = activations.reshape(step_count, block_count, BLOCK, width_dev)
    rank_part = jnp.einsum("sbkd,bdr->sbkr", blocked, down, preferred_element_type=jnp.float32)
    rank_sum = lax.psum(rank_part, "tensor")
    base = base_sum(
        activations.reshape(step_count * row_count, width_dev), shared_weight_matrix, length
    )
    rank_scaled = (rank_sum * scale.astype(jnp.float32)[None, :, None, :]).astype(jnp.bfloat16)
    delta = jnp.einsum("sbkr,brc->sbkc", rank_scaled, up, preferred_element_type=jnp.float32)
    projected = base.reshape(delta.shape) + delta
    return projected.astype(jnp.bfloat16).reshape(activations.shape)


def solution(mesh):
    in_specs = (
        P(None, ("parts", "serve"), "tensor"),
        P("tensor", None),
        P("serve", "tensor", None),
        P("serve", None, "tensor"),
        P("serve", None),
        P("parts"),
    )
    out_specs = P(None, ("parts", "serve"), "tensor")
    return jax.shard_map(
        functools.partial(per_device, mesh.shape["tensor"] // 2),
        mesh=mesh,
        in_specs=in_specs,
        out_specs=out_specs,
        check_vma=False,
    )
```

```python
import functools

import jax
import jax.numpy as jnp
from jax import lax
from jax.experimental import pallas as pl
from jax.experimental.pallas import tpu as pltpu
from jax.sharding import PartitionSpec as P

BLOCK = 128
MESH = pl.DeviceIdType.MESH


def chunk_at(step, place, length):
    after, before = length - 1 - place, place
    fewer = jnp.minimum(after, before)
    after_more = after > before
    interleaved = step < 2 * fewer
    count = jnp.where(interleaved, step // 2, step - fewer)
    goes_after = jnp.where(interleaved & (step % 2 == 1), jnp.logical_not(after_more), after_more)
    chunk = jnp.where(goes_after, length - 1 - count, count)
    return jnp.where(step == length - 1, place, chunk)


def project_kernel(
    length,
    x_ref,
    w_ref,
    rank_ref,
    scale_ref,
    up_ref,
    out_ref,
    x_pair,
    w_own,
    w_pair,
    acc,
    rank_pair,
    rank_out,
    rank_in,
    own_sem,
    x_send,
    x_recv,
    y_send,
    y_recv,
    across_send,
    across_recv,
    core_send,
    core_recv,
    chain_send,
    chain_recv,
    rank_send,
    rank_recv,
):
    tiles, rows, width = x_ref.shape
    blocks = up_ref.shape[0]
    part, group, index = lax.axis_index("parts"), lax.axis_index("serve"), lax.axis_index("tensor")
    side, place = index % 2, index // 2
    twin = index + 1 - 2 * side
    other_part = part + 1 - 2 * (part % 2)
    other_group = 1 - group
    quarter = width // 4
    mine = pl.multiple_of((2 * (part % 2) + group) * quarter, quarter)
    across = pl.multiple_of((2 * (other_part % 2) + group) * quarter, quarter)

    def columns(chunk, which):
        return pl.ds(pl.multiple_of((2 * chunk + which) * width, width), width)

    def own_copy(step):
        chunk = chunk_at(step, place, length)
        return pltpu.make_async_copy(
            w_ref.at[:, columns(chunk, side)], w_own.at[chunk], own_sem.at[chunk]
        )

    def x_copy(tile):
        return pltpu.make_async_remote_copy(
            src_ref=x_ref.at[tile],
            dst_ref=x_pair.at[tile],
            send_sem=x_send.at[tile],
            recv_sem=x_recv.at[tile],
            device_id={"tensor": twin},
            device_id_type=MESH,
        )

    def y_copy(step):
        chunk = chunk_at(step, place, length)
        return pltpu.make_async_remote_copy(
            src_ref=w_ref.at[pl.ds(mine, quarter), columns(chunk, 1 - side)],
            dst_ref=w_pair.at[chunk, pl.ds(mine, quarter), :],
            send_sem=y_send.at[chunk],
            recv_sem=y_recv.at[chunk],
            device_id={"tensor": twin},
            device_id_type=MESH,
        )

    def across_copy(step):
        chunk = chunk_at(step, place, length)
        block = w_pair.at[chunk, pl.ds(mine, quarter), :]
        return pltpu.make_async_remote_copy(
            src_ref=block,
            dst_ref=block,
            send_sem=across_send.at[chunk],
            recv_sem=across_recv.at[chunk],
            device_id={"parts": other_part},
            device_id_type=MESH,
        )

    def core_copy(step, which, start):
        chunk = chunk_at(step, place, length)
        block = w_pair.at[chunk, pl.ds(start, quarter), :]
        return pltpu.make_async_remote_copy(
            src_ref=block,
            dst_ref=block,
            send_sem=core_send.at[which, chunk],
            recv_sem=core_recv.at[which, chunk],
            device_id={"serve": other_group},
            device_id_type=MESH,
        )

    def chain_copy(chunk, tile, slot, target):
        return pltpu.make_async_remote_copy(
            src_ref=acc.at[chunk, tile],
            dst_ref=acc.at[slot, tile],
            send_sem=chain_send.at[chunk, tile],
            recv_sem=chain_recv.at[slot, tile],
            device_id={"tensor": target},
            device_id_type=MESH,
        )

    def rank_copy(which, target):
        return pltpu.make_async_remote_copy(
            src_ref=rank_out.at[which],
            dst_ref=rank_in.at[which],
            send_sem=rank_send.at[which],
            recv_sem=rank_recv.at[which],
            device_id={"tensor": target},
            device_id_type=MESH,
        )

    def rank_along_chain():
        rank_copy(0, index).wait_recv()
        rank_pair[...] = rank_ref[...] + rank_in[0].astype(jnp.float32)

        @pl.when(place == 0)
        def _():
            rank_in[1] = jnp.zeros_like(rank_in[1])

        @pl.when(place == length - 1)
        def _():
            rank_in[2] = jnp.zeros_like(rank_in[2])

        @pl.when(place > 0)
        def _():
            rank_copy(1, index).wait_recv()

        @pl.when(place < length - 1)
        def _():
            rank_out[1] = (rank_pair[...] + rank_in[1].astype(jnp.float32)).astype(rank_out.dtype)
            rank_copy(1, index + 2).start()
            rank_copy(2, index).wait_recv()

        @pl.when(place > 0)
        def _():
            rank_out[2] = (rank_pair[...] + rank_in[2].astype(jnp.float32)).astype(rank_out.dtype)
            rank_copy(2, index - 2).start()

        rank_pair[...] += rank_in[1].astype(jnp.float32) + rank_in[2].astype(jnp.float32)

    def forward_first(step):
        y_copy(step).wait_recv()
        across_copy(step).start()
        core_copy(step, 0, mine).start()

    def forward_second(step):
        across_copy(step).wait_recv()
        core_copy(step, 1, across).start()

    @pl.loop(0, length)
    def _(step):
        own_copy(step).start()

    rank_out[0] = rank_ref[...].astype(rank_out.dtype)

    barrier = pltpu.get_barrier_semaphore()
    pl.semaphore_signal(barrier, inc=1, device_id={"tensor": twin}, device_id_type=MESH)
    pl.semaphore_signal(barrier, inc=1, device_id={"parts": other_part}, device_id_type=MESH)
    pl.semaphore_signal(barrier, inc=1, device_id={"serve": other_group}, device_id_type=MESH)

    @pl.when(place > 0)
    def _():
        pl.semaphore_signal(barrier, inc=1, device_id={"tensor": index - 2}, device_id_type=MESH)

    @pl.when(place < length - 1)
    def _():
        pl.semaphore_signal(barrier, inc=1, device_id={"tensor": index + 2}, device_id_type=MESH)

    at_end = (place == 0) | (place == length - 1)
    pl.semaphore_wait(barrier, jnp.where(at_end, 4, 5))

    rank_copy(0, twin).start()
    y_copy(0).start()

    @pl.loop(0, tiles)
    def _(tile):
        x_copy(tile).start()

    @pl.loop(1, length)
    def _(step):
        y_copy(step).start()

    rank_along_chain()
    forward_first(0)
    forward_second(0)

    @pl.loop(0, length)
    def _(step):
        chunk = chunk_at(step, place, length)
        own_copy(step).wait()
        core_copy(step, 0, mine).wait_recv()
        core_copy(step, 1, across).wait_recv()

        @pl.loop(0, tiles)
        def _(tile):
            @pl.when(step == 0)
            def _():
                x_copy(tile).wait_recv()

            part_sum = jnp.dot(
                x_ref[tile], w_own[chunk], preferred_element_type=jnp.float32
            ) + jnp.dot(x_pair[tile], w_pair[chunk], preferred_element_type=jnp.float32)

            @pl.when(chunk == place)
            def _():
                block = tile % blocks
                scaled = (rank_pair[tile] * scale_ref[block].astype(jnp.float32)).astype(
                    jnp.bfloat16
                )
                whole = part_sum + jnp.dot(
                    scaled, up_ref[block], preferred_element_type=jnp.float32
                )

                @pl.when(place == 0)
                def _():
                    acc[chunk, tile] = jnp.zeros_like(acc[chunk, tile])

                @pl.when(place == length - 1)
                def _():
                    acc[length, tile] = jnp.zeros_like(acc[length, tile])

                @pl.when(place > 0)
                def _():
                    chain_copy(chunk, tile, chunk, index).wait_recv()

                @pl.when(place < length - 1)
                def _():
                    chain_copy(chunk, tile, length, index).wait_recv()

                out_ref[tile] = (
                    whole
                    + acc[chunk, tile].astype(jnp.float32)
                    + acc[length, tile].astype(jnp.float32)
                ).astype(out_ref.dtype)

            @pl.when(chunk != place)
            def _():
                up = chunk > place
                first = jnp.where(up, place == 0, place == length - 1)

                @pl.when(first)
                def _():
                    acc[chunk, tile] = part_sum.astype(acc.dtype)

                @pl.when(jnp.logical_not(first))
                def _():
                    chain_copy(chunk, tile, chunk, index).wait_recv()
                    acc[chunk, tile] = (part_sum + acc[chunk, tile].astype(jnp.float32)).astype(
                        acc.dtype
                    )

                target = jnp.where(up, index + 2, index - 2)
                slot = jnp.where(chunk == place - 1, length, chunk)
                chain_copy(chunk, tile, slot, target).start()

            @pl.when((step < length - 1) & (tile == jnp.where(step == 0, tiles - 1, tiles // 2)))
            def _():
                forward_first(step + 1)

            @pl.when((step < length - 1) & (tile == tiles - 1))
            def _():
                forward_second(step + 1)

    rank_copy(0, index).wait_send()

    @pl.when(place < length - 1)
    def _():
        rank_copy(1, index).wait_send()

    @pl.when(place > 0)
    def _():
        rank_copy(2, index).wait_send()

    @pl.loop(0, tiles)
    def _(tile):
        x_copy(tile).wait_send()

    @pl.loop(0, length)
    def _(step):
        y_copy(step).wait_send()
        across_copy(step).wait_send()
        core_copy(step, 0, mine).wait_send()
        core_copy(step, 1, across).wait_send()

        chunk = chunk_at(step, place, length)

        @pl.when(chunk != place)
        def _():
            @pl.loop(0, tiles)
            def _(tile):
                chain_copy(chunk, tile, chunk, index).wait_send()


def project(activations, shared_weight_matrix, rank_part, scale, up, length):
    row_count, width = activations.shape
    tiles = row_count // BLOCK
    rank = rank_part.shape[-1]
    dma = pltpu.SemaphoreType.DMA
    return pl.pallas_call(
        functools.partial(project_kernel, length),
        out_shape=jax.ShapeDtypeStruct((tiles, BLOCK, width), jnp.bfloat16),
        in_specs=[
            pl.BlockSpec(memory_space=pltpu.VMEM),
            pl.BlockSpec(memory_space=pl.ANY),
            pl.BlockSpec(memory_space=pltpu.VMEM),
            pl.BlockSpec(memory_space=pltpu.VMEM),
            pl.BlockSpec(memory_space=pltpu.VMEM),
        ],
        out_specs=pl.BlockSpec(memory_space=pltpu.VMEM),
        scratch_shapes=[
            pltpu.VMEM((tiles, BLOCK, width), jnp.bfloat16),
            pltpu.VMEM((length, width, width), jnp.bfloat16),
            pltpu.VMEM((length, width, width), jnp.bfloat16),
            pltpu.VMEM((length + 1, tiles, BLOCK, width), jnp.bfloat16),
            pltpu.VMEM((tiles, BLOCK, rank), jnp.float32),
            pltpu.VMEM((3, tiles, BLOCK, rank), jnp.bfloat16),
            pltpu.VMEM((3, tiles, BLOCK, rank), jnp.bfloat16),
            dma((length,)),
            dma((tiles,)),
            dma((tiles,)),
            dma((length,)),
            dma((length,)),
            dma((length,)),
            dma((length,)),
            dma((2, length)),
            dma((2, length)),
            dma((length, tiles)),
            dma((length + 1, tiles)),
            dma((3,)),
            dma((3,)),
        ],
        compiler_params=pltpu.CompilerParams(
            collective_id=0, has_side_effects=True, vmem_limit_bytes=52 * 2**20
        ),
        cost_estimate=pl.CostEstimate(
            flops=4 * row_count * width * width * length * 8,
            bytes_accessed=2 * width * width * length * 2 * 8,
            transcendentals=0,
        ),
        name="project",
    )(
        activations.reshape(tiles, BLOCK, width),
        shared_weight_matrix,
        rank_part.reshape(tiles, BLOCK, rank),
        scale[:, None, :],
        up,
    )


def pick_rows(table, served, group_index):
    held = table.shape[0]
    count = served.shape[0] // 2
    local = served - group_index * held
    here = (local >= 0) & (local < held)
    local = jnp.clip(local, 0, held - 1)
    ours = lax.dynamic_slice_in_dim(local, group_index * count, count)
    ours_here = lax.dynamic_slice_in_dim(here, group_index * count, count)
    theirs = lax.dynamic_slice_in_dim(local, (1 - group_index) * count, count)
    sent = jnp.take(table, theirs, axis=0)
    arrived = lax.ppermute(sent, "serve", [(0, 1), (1, 0)])
    kept = jnp.take(table, ours, axis=0)
    shape = (count,) + (1,) * (table.ndim - 1)
    return jnp.where(ours_here.reshape(shape), kept, arrived)


def per_device(
    length,
    activations,
    shared_weight_matrix,
    adapter_down_weight,
    adapter_up_weight,
    adapter_rank_scale,
    block_adapter_index,
):
    step_count, row_count, width_dev = activations.shape
    block_count = row_count // BLOCK
    group_index = lax.axis_index("serve")
    down = pick_rows(adapter_down_weight, block_adapter_index, group_index)
    up = pick_rows(adapter_up_weight, block_adapter_index, group_index)
    scale = pick_rows(adapter_rank_scale, block_adapter_index, group_index)
    blocked = activations.reshape(step_count, block_count, BLOCK, width_dev)
    rank_part = jnp.einsum("sbkd,bdr->sbkr", blocked, down, preferred_element_type=jnp.float32)
    projected = project(
        activations.reshape(step_count * row_count, width_dev),
        shared_weight_matrix,
        rank_part,
        scale,
        up,
        length,
    )
    return projected.reshape(activations.shape)


def solution(mesh):
    in_specs = (
        P(None, ("parts", "serve"), "tensor"),
        P("tensor", None),
        P("serve", "tensor", None),
        P("serve", None, "tensor"),
        P("serve", None),
        P("parts"),
    )
    out_specs = P(None, ("parts", "serve"), "tensor")
    return jax.shard_map(
        functools.partial(per_device, mesh.shape["tensor"] // 2),
        mesh=mesh,
        in_specs=in_specs,
        out_specs=out_specs,
        check_vma=False,
    )
```
